512 devices in a mesh: seq: 32 (over z, core), cache: 16 (over y, x).
Axes of the slice: x: 4, y: 4, z: 16, core: 2. Of those that a mesh axis runs over, the one named last changes fastest.
Arguments:
- qkv: bfloat16 [16, 1536, 3, 4096], P('cache', 'seq'), may hold values from -6 to 6
- cache_kv: bfloat16 [32, 2, 256, 4096], P('cache', None, None, 'seq'), may hold values from -6 to 6
- group_list: int32 [16, 15], P('cache'), may hold values from 0 to 31, as said below
- stream_counts: int32 [16], P('cache'), may hold values from 1 to 15
Outputs:
- attended: bfloat16 [16, 1536, 4096], P('cache', 'seq')
The draws below stay inside these ranges and needn't reach their ends.
Inputs may be any that keep to these rules, and one draw needn't show every extreme that they name: `group_list`: only the first stream_counts[s] entries of row s are used. The 15 ids of one row lie with different indices of cache: no two share id // 2.
All inputs are finite; a program needn't handle non-finite values.
Results may differ from the reference program's by a relative error of at most 0.006.
Values may be sent and summed in bfloat16 or wider, within the bound.
A program may use at most 64 MiB of HBM per device.

```python
import math
import jax
import jax.numpy as jnp
from jax import lax

HEAD = 128
HEADS = 32
FTOK = 256
POOL_DEV = 2
LIST = 15
GROUP = 1536
STREAMS = 16
POOL = 32


def draw_qkv(key, part):
    key = jax.random.fold_in(key, 11)
    subkeys = jax.random.split(key, 1)
    full_shape = (STREAMS, GROUP, 3, HEADS * HEAD)
    stacked = jnp.clip(jax.random.normal(subkeys[0], full_shape, jnp.float32), -4.0, 4.0)
    return stacked.astype(jnp.bfloat16)


def draw_group_list(key, part):
    key = jax.random.fold_in(key, 21)
    subkeys = jax.random.split(key, 3)
    stream_keys = jax.random.split(subkeys[0], STREAMS)
    holders = jax.vmap(lambda one_key: jax.random.permutation(one_key, STREAMS)[:LIST])(stream_keys).astype(jnp.int32)
    offsets = jax.random.randint(subkeys[1], (STREAMS, LIST), 0, POOL_DEV)
    chosen = jax.random.randint(subkeys[2], (), 0, STREAMS)
    second = (chosen + 1) % STREAMS
    streams = jnp.arange(STREAMS)[:, None]
    top_shift = (holders - holders[:, :1] + STREAMS - 1) % STREAMS
    low_shift = (holders - holders[:, :1] + STREAMS) % STREAMS
    holders = jnp.where(streams == chosen, top_shift, jnp.where(streams == second, low_shift, holders))
    first_slot = jnp.arange(LIST)[None, :] == 0
    offsets = jnp.where((streams == chosen) & first_slot, POOL_DEV - 1, jnp.where((streams == second) & first_slot, 0, offsets))
    return (holders * POOL_DEV + offsets).astype(jnp.int32)


def draw_stream_counts(key, part):
    key = jax.random.fold_in(key, 31)
    subkeys = jax.random.split(key, 2)
    drawn = jax.random.randint(subkeys[0], (STREAMS,), 1, LIST + 1)
    chosen = jax.random.randint(subkeys[1], (), 0, STREAMS)
    return jnp.where(jnp.arange(STREAMS) == chosen, LIST, drawn).astype(jnp.int32)


def shard_levels(stream_key, dims, pieces, low, largest):
    loudness = 1.0
    for axis_at, shards_of in pieces:
        heights = jax.random.uniform(jax.random.fold_in(jax.random.fold_in(stream_key, 6), axis_at), (shards_of,), jnp.float32, low / len(pieces), largest / len(pieces))
        loudness = loudness * jnp.repeat(jnp.exp(heights), dims[axis_at] // shards_of).reshape((-1,) + (1,) * (len(dims) - 1 - axis_at))
    return loudness


def bell_draw(key, dims, spread, bound, pieces=(), kind=jnp.bfloat16):
    values = spread * jax.random.normal(key, dims, jnp.float32)
    if pieces:
        values = values * shard_levels(key, dims, pieces, -0.22, 0.18)
    return jnp.clip(values, -bound, bound).astype(kind)


def setup_inputs(seed: int = 0) -> dict:
    streams_of = jax.random.split(jax.random.key(seed), 5)
    qkv = draw_qkv(jax.random.fold_in(streams_of[4], 71), 0)
    cache_kv = bell_draw(streams_of[1], (POOL, 2, FTOK, HEADS * HEAD), 1.0, 6.0, ((0, 16), (3, 32)))
    group_list = draw_group_list(jax.random.fold_in(streams_of[4], 71), 0)
    stream_counts = draw_stream_counts(jax.random.fold_in(streams_of[4], 71), 0)
    return {"qkv": qkv, "cache_kv": cache_kv, "group_list": group_list, "stream_counts": stream_counts}


MASKED_SCORE = -1e+30

def absorb(running, queries, key_rows, value_rows, visible):
    row_peak, row_total, weighted = running
    scores = jnp.dot(queries, key_rows.T, preferred_element_type=jnp.float32) / math.sqrt(queries.shape[-1])
    if visible is not None:
        scores = jnp.where(visible, scores, MASKED_SCORE)
    raised = jnp.maximum(row_peak, lax.optimization_barrier(jnp.max(scores, axis=1)))
    rescale = jnp.exp(row_peak - raised)
    weights = jnp.exp(scores - raised[:, None]).astype(jnp.bfloat16)
    row_total = rescale * row_total + lax.optimization_barrier(jnp.sum(weights.astype(jnp.float32), axis=1))
    weighted = rescale[:, None] * weighted + jnp.dot(weights, value_rows, preferred_element_type=jnp.float32)
    return (raised, row_total, weighted)

def one_head(queries, key_rows, value_rows, cached, slot_count):
    group_len = queries.shape[0]
    frames = jnp.arange(group_len) // FTOK
    visible = frames[None, :] <= frames[:, None]
    running = (jnp.full((group_len,), MASKED_SCORE, jnp.float32), jnp.zeros((group_len,), jnp.float32), jnp.zeros(queries.shape, jnp.float32))
    running = absorb(running, queries, key_rows, value_rows, visible)
    for slot in range(cached.shape[0]):
        updated = absorb(running, queries, cached[slot, 0], cached[slot, 1], None)
        running = jax.tree.map(lambda new_v, old_v: jnp.where(slot < slot_count, new_v, old_v), updated, running)
    row_peak, row_total, weighted = running
    return (weighted / row_total[:, None]).astype(jnp.bfloat16)

def reference(qkv, cache_kv, group_list, stream_counts):

    def per_stream(inputs):
        stream_rows, slot_ids, slot_count = inputs
        blocks = jnp.take(cache_kv, slot_ids.astype(jnp.int32), axis=0)
        rows_heads = jnp.moveaxis(stream_rows.reshape(GROUP, 3, HEADS, HEAD), 2, 0)
        blocks_heads = jnp.moveaxis(blocks.reshape(LIST, 2, FTOK, HEADS, HEAD), 3, 0)

        def per_head(pair):
            head_rows, head_blocks = pair
            return one_head(head_rows[:, 0], head_rows[:, 1], head_rows[:, 2], head_blocks, slot_count)
        per_heads = lax.map(per_head, (rows_heads, blocks_heads))
        return jnp.moveaxis(per_heads, 0, 1).reshape(GROUP, HEADS * HEAD)
    return lax.map(per_stream, (qkv, group_list, stream_counts))
```

```python
import math

import jax
import jax.numpy as jnp
from jax import lax
from jax.experimental import pallas as pl
from jax.experimental.pallas import tpu as pltpu
from jax.sharding import PartitionSpec as P

HEAD = 128
FTOK = 256
CHUNK = 3
ROWS = 512
MESH = pl.DeviceIdType.MESH
RATE = math.log2(math.e) / math.sqrt(HEAD)
LOWEST = -3.0e38


def rows_dot(a, b):
    return lax.dot_general(a, b, (((1,), (1,)), ((), ())), preferred_element_type=jnp.float32)


def kernel(sizes, list_ref, count_ref, x_ref, cache_ref, out_ref, q_buf, k_buf, v_buf, o_buf,
           note, notes, c_send, c_buf, k_all, v_all, peak, acc, weights,
           note_ssem, note_rsem, c_ssem, c_rsem, q_ssem, q_rsem, k_ssem, k_rsem, v_ssem, v_rsem,
           o_ssem, o_rsem):
    n_seq, n_cache, tok, slots, side = sizes
    n_z = n_seq // 2
    s = lax.axis_index("seq")
    c = lax.axis_index("cache")
    z, core = s // 2, s % 2
    cy, cx = c // side, c % side
    group = n_seq * tok
    frames = group // FTOK

    def seq_peer(i):
        step = i // 2
        far = n_z // 2 - (step + 1) // 2
        dz = jnp.where(step % 2 == 1, far, n_z - far)
        return lax.rem(z + dz, n_z) * 2 + lax.rem(core + i + 1, 2)

    def cache_peer(i):
        return lax.rem(cy + i // side, side) * side + lax.rem(cx + lax.rem(i, side), side)

    def head_cols(p):
        return pl.ds(pl.multiple_of(p * HEAD, HEAD), HEAD)

    def tok_rows(p):
        return pl.ds(pl.multiple_of(p * tok, 16), tok)

    barrier = pltpu.get_barrier_semaphore()

    @pl.loop(0, n_seq - 1)
    def _(i):
        pl.semaphore_signal(barrier, inc=1, device_id={"seq": seq_peer(i)}, device_id_type=MESH)

    @pl.loop(1, n_cache)
    def _(i):
        pl.semaphore_signal(barrier, inc=1, device_id={"cache": cache_peer(i)}, device_id_type=MESH)

    lanes = lax.broadcasted_iota(jnp.int32, (8, 128), 1)
    row = jnp.full((8, 128), -1, jnp.int32)
    used = count_ref[0]
    for j in range(slots):
        row = jnp.where(lanes == j, jnp.where(j < used, list_ref[0, j], -1), row)
    note[...] = row
    notes[c] = row
    q_buf[tok_rows(s), :] = x_ref[0, :, head_cols(s)]
    k_buf[tok_rows(s), :] = x_ref[1, :, head_cols(s)]
    v_buf[tok_rows(s), 0:HEAD] = x_ref[2, :, head_cols(s)]
    v_buf[:, HEAD:2 * HEAD] = jnp.ones((group, HEAD), jnp.bfloat16)

    pl.semaphore_wait(barrier, n_seq - 1 + n_cache - 1)

    @pl.loop(1, n_cache)
    def _(i):
        pltpu.make_async_remote_copy(note, notes.at[c], note_ssem, note_rsem,
                                     device_id={"cache": cache_peer(i)}, device_id_type=MESH).start()

    def send_part(part, dst, ssem, rsem):
        @pl.loop(0, n_seq - 1)
        def _(i):
            p = seq_peer(i)
            pltpu.make_async_remote_copy(x_ref.at[part, :, head_cols(p)], dst, ssem, rsem,
                                         device_id={"seq": p}, device_id_type=MESH).start()

    send_part(0, q_buf.at[tok_rows(s), :], q_ssem, q_rsem)

    others = n_cache - 1
    pltpu.make_async_copy(notes.at[pl.ds(0, others)], notes.at[pl.ds(0, others)], note_rsem).wait()
    pltpu.make_async_copy(notes.at[pl.ds(0, others)], notes.at[pl.ds(0, others)], note_ssem).wait()

    def listed(p):
        hit = jnp.where(notes[p] == 2 * c + 1, 1, 0)
        return jnp.max(hit)

    @pl.loop(1, n_cache)
    def _(i):
        p = cache_peer(i)
        c_send[p] = cache_ref[listed(p)]
        pltpu.make_async_remote_copy(c_send.at[p], c_buf.at[c], c_ssem, c_rsem,
                                     device_id={"cache": p}, device_id_type=MESH).start()

    c_buf[c] = cache_ref[listed(c)]
    send_part(1, k_buf.at[tok_rows(s), :], k_ssem, k_rsem)
    send_part(2, v_buf.at[tok_rows(s), 0:HEAD], v_ssem, v_rsem)

    far_rows = group - tok

    def wait_part(ref, sem):
        pltpu.make_async_copy(ref, ref, sem).wait()

    wait_part(q_buf.at[0:far_rows], q_rsem)
    wait_part(c_buf.at[pl.ds(0, others)], c_rsem)

    @pl.loop(0, slots)
    def _(j):
        valid = j < used
        at = jnp.where(valid, list_ref[0, j], list_ref[0, 0]) // 2
        keep = jnp.where(valid, 1.0, 0.0).astype(jnp.float32)
        rows = pl.ds(pl.multiple_of(j * FTOK, FTOK), FTOK)
        k_all[rows, :] = c_buf[at, 0]
        v_all[rows, 0:HEAD] = (c_buf[at, 1].astype(jnp.float32) * keep).astype(jnp.bfloat16)
        v_all[rows, HEAD:2 * HEAD] = jnp.full((FTOK, HEAD), keep, jnp.float32).astype(jnp.bfloat16)

    @pl.loop(0, group // ROWS)
    def _(t):
        rows = pl.ds(pl.multiple_of(t * ROWS, ROWS), ROWS)
        queries = q_buf[rows, :]

        def step(j, carry):
            top, total = carry
            keys = pl.ds(pl.multiple_of(j * CHUNK * FTOK, FTOK), CHUNK * FTOK)
            scores = rows_dot(queries, k_all[keys, :])
            raised = jnp.maximum(top, jnp.max(scores, axis=1, keepdims=True))
            fade = jnp.exp2((top - raised) * RATE)
            w = jnp.exp2((scores - raised) * RATE).astype(jnp.bfloat16)
            total = total * fade + jnp.dot(w, v_all[keys, :], preferred_element_type=jnp.float32)
            return raised, total

        top, total = lax.fori_loop(
            0, slots // CHUNK, step,
            (jnp.full((ROWS, 1), LOWEST, jnp.float32), jnp.zeros((ROWS, 2 * HEAD), jnp.float32)))
        peak[rows, :] = jnp.broadcast_to(top, (ROWS, HEAD))
        acc[rows, :] = total

    wait_part(k_buf.at[0:far_rows], k_rsem)
    for f in range(frames):
        rows = slice(f * FTOK, (f + 1) * FTOK)
        top = peak[rows, 0:1]
        seen = (f + 1) * FTOK
        scores = rows_dot(q_buf[rows, :], k_buf[0:seen, :])
        raised = jnp.maximum(top, jnp.max(scores, axis=1, keepdims=True))
        weights[rows, 0:seen] = jnp.exp2((scores - raised) * RATE).astype(jnp.bfloat16)
        acc[rows, :] = acc[rows, :] * jnp.exp2((top - raised) * RATE)

    wait_part(v_buf.at[0:far_rows, 0:HEAD], v_rsem)
    for f in range(frames):
        rows = slice(f * FTOK, (f + 1) * FTOK)
        seen = (f + 1) * FTOK
        total = acc[rows, :] + jnp.dot(weights[rows, 0:seen], v_buf[0:seen, :], preferred_element_type=jnp.float32)
        o_buf[rows, :] = (total[:, 0:HEAD] / total[:, HEAD:2 * HEAD]).astype(jnp.bfloat16)

    @pl.loop(0, n_seq - 1)
    def _(i):
        p = seq_peer(i)
        pltpu.make_async_remote_copy(o_buf.at[tok_rows(p), :], out_ref.at[:, head_cols(s)], o_ssem, o_rsem,
                                     device_id={"seq": p}, device_id_type=MESH).start()

    out_ref[:, head_cols(s)] = o_buf[tok_rows(s), :]
    wait_part(q_buf.at[0:far_rows], q_ssem)
    wait_part(k_buf.at[0:far_rows], k_ssem)
    wait_part(v_buf.at[0:far_rows, 0:HEAD], v_ssem)
    wait_part(c_buf.at[pl.ds(0, others)], c_ssem)
    wait_part(o_buf.at[0:far_rows], o_ssem)
    wait_part(o_buf.at[0:far_rows], o_rsem)


def solution(mesh):
    n_seq, n_cache = mesh.shape["seq"], mesh.shape["cache"]
    side = math.isqrt(n_cache)

    def shards(qkv, cache_kv, group_list, stream_counts):
        parts = jnp.transpose(qkv[0], (1, 0, 2))
        tok, width = parts.shape[1], parts.shape[2]
        slots = group_list.shape[1]
        group = tok * n_seq
        bf16, f32 = jnp.bfloat16, jnp.float32
        vmem = pl.BlockSpec(memory_space=pltpu.VMEM)
        smem = pl.BlockSpec(memory_space=pltpu.SMEM)

        def body(*refs):
            kernel((n_seq, n_cache, tok, slots, side), *refs)

        out = pl.pallas_call(
            body,
            out_shape=jax.ShapeDtypeStruct((tok, width), bf16),
            in_specs=[smem, smem, vmem, vmem],
            out_specs=vmem,
            scratch_shapes=[
                pltpu.VMEM((group, HEAD), bf16),
                pltpu.VMEM((group, HEAD), bf16),
                pltpu.VMEM((group, 2 * HEAD), bf16),
                pltpu.VMEM((group, HEAD), bf16),
                pltpu.VMEM((8, 128), jnp.int32),
                pltpu.VMEM((n_cache, 8, 128), jnp.int32),
                pltpu.VMEM((n_cache, 2, FTOK, HEAD), bf16),
                pltpu.VMEM((n_cache, 2, FTOK, HEAD), bf16),
                pltpu.VMEM((slots * FTOK, HEAD), bf16),
                pltpu.VMEM((slots * FTOK, 2 * HEAD), bf16),
                pltpu.VMEM((group, HEAD), f32),
                pltpu.VMEM((group, 2 * HEAD), f32),
                pltpu.VMEM((group, group), bf16),
            ] + [pltpu.SemaphoreType.DMA] * 12,
            compiler_params=pltpu.CompilerParams(
                collective_id=0, has_side_effects=True, vmem_limit_bytes=56 << 20),
            cost_estimate=pl.CostEstimate(
                flops=4 * group * (group + slots * FTOK) * HEAD,
                bytes_accessed=4 * tok * width * 2 + 4 * FTOK * HEAD * 2,
                transcendentals=group * (group + slots * FTOK)),
        )(group_list, stream_counts, parts, cache_kv)
        return out[None]

    placed = (
        P("cache", "seq", None, None),
        P("cache", None, None, "seq"),
        P("cache", None),
        P("cache"),
    )
    return jax.shard_map(
        shards, mesh=mesh, in_specs=placed, out_specs=P("cache", "seq", None), check_vma=False
    )
```

```python
import math

import jax
import jax.numpy as jnp
from jax import lax
from jax.experimental import pallas as pl
from jax.experimental.pallas import tpu as pltpu
from jax.sharding import PartitionSpec as P

HEAD = 128
FTOK = 256
MESH = pl.DeviceIdType.MESH
RATE = math.log2(math.e) / math.sqrt(HEAD)
LOWEST = -3.0e38


def rows_dot(a, b):
    return lax.dot_general(a, b, (((1,), (1,)), ((), ())), preferred_element_type=jnp.float32)


def kernel(sizes, list_hbm, count_hbm, x_ref, cache_ref, out_ref, q_buf, k_buf, v_buf, o_buf,
           list_ref, count_ref, note, notes, c_mine, c_send, c_buf, k_all, v_all, scored, own_scored, acc, weights,
           own_sem, note_ssem, note_rsem, c_ssem, c_rsem, q_ssem, q_rsem, k_ssem, k_rsem, v_ssem, v_rsem,
           o_ssem, o_rsem):
    n_seq, n_cache, tok, slots, side = sizes
    n_z = n_seq // 2
    s = lax.axis_index("seq")
    c = lax.axis_index("cache")
    z, core = s // 2, s % 2
    cy, cx = c // side, c % side
    group = n_seq * tok
    frames = group // FTOK

    def seq_peer(i):
        step = i // 2
        far = n_z // 2 - (step + 1) // 2
        dz = jnp.where(step % 2 == 1, far, n_z - far)
        return lax.rem(z + dz, n_z) * 2 + lax.rem(core + i + 1, 2)

    def cache_peer(i):
        return lax.rem(cy + i // side, side) * side + lax.rem(cx + lax.rem(i, side), side)

    def head_cols(p):
        return pl.ds(pl.multiple_of(p * HEAD, HEAD), HEAD)

    def tok_rows(p):
        return pl.ds(pl.multiple_of(p * tok, 16), tok)

    barrier = pltpu.get_barrier_semaphore()

    @pl.loop(0, n_seq - 1)
    def _(i):
        pl.semaphore_signal(barrier, inc=1, device_id={"seq": seq_peer(i)}, device_id_type=MESH)

    @pl.loop(1, n_cache)
    def _(i):
        pl.semaphore_signal(barrier, inc=1, device_id={"cache": cache_peer(i)}, device_id_type=MESH)

    lists = [pltpu.make_async_copy(list_hbm, list_ref, own_sem.at[4]), pltpu.make_async_copy(count_hbm, count_ref, own_sem.at[5])]
    for copy in lists:
        copy.start()

    mine = [
        pltpu.make_async_copy(cache_ref, c_mine, own_sem.at[0]),
        pltpu.make_async_copy(x_ref.at[0, :, head_cols(s)], q_buf.at[tok_rows(s), :], own_sem.at[1]),
        pltpu.make_async_copy(x_ref.at[1, :, head_cols(s)], k_buf.at[tok_rows(s), :], own_sem.at[2]),
        pltpu.make_async_copy(x_ref.at[2, :, head_cols(s)], v_buf.at[tok_rows(s), 0:HEAD], own_sem.at[3]),
    ]
    for copy in mine:
        copy.start()

    for copy in lists:
        copy.wait()
    lanes = lax.broadcasted_iota(jnp.int32, (8, 128), 1)
    row = jnp.full((8, 128), -1, jnp.int32)
    used = count_ref[0]
    for j in range(slots):
        row = jnp.where(lanes == j, jnp.where(j < used, list_ref[0, j], -1), row)
    note[...] = row
    notes[c] = row
    v_buf[:, HEAD:2 * HEAD] = jnp.ones((group, HEAD), jnp.bfloat16)

    pl.semaphore_wait(barrier, n_seq - 1 + n_cache - 1)

    @pl.loop(1, n_cache)
    def _(i):
        pltpu.make_async_remote_copy(note, notes.at[c], note_ssem, note_rsem,
                                     device_id={"cache": cache_peer(i)}, device_id_type=MESH).start()

    def send_part(part, dst, ssem, rsem, in_turn=False):
        @pl.loop(0, n_seq - 1)
        def _(i):
            p = jnp.where(i < s, i, i + 1) if in_turn else seq_peer(i)
            pltpu.make_async_remote_copy(x_ref.at[part, :, head_cols(p)], dst, ssem, rsem,
                                         device_id={"seq": p}, device_id_type=MESH).start()

    send_part(0, q_buf.at[tok_rows(s), :], q_ssem, q_rsem)

    for copy in mine:
        copy.wait()
    others = n_cache - 1
    pltpu.make_async_copy(notes.at[pl.ds(0, others)], notes.at[pl.ds(0, others)], note_rsem).wait()
    pltpu.make_async_copy(notes.at[pl.ds(0, others)], notes.at[pl.ds(0, others)], note_ssem).wait()

    def listed(p):
        hit = jnp.where(notes[p] == 2 * c + 1, 1, 0)
        return jnp.max(hit)

    @pl.loop(1, n_cache)
    def _(i):
        p = cache_peer(i)
        c_send[p] = c_mine[listed(p)]
        pltpu.make_async_remote_copy(c_send.at[p], c_buf.at[c], c_ssem, c_rsem,
                                     device_id={"cache": p}, device_id_type=MESH).start()

    c_buf[c] = c_mine[listed(c)]
    send_part(1, k_buf.at[tok_rows(s), :], k_ssem, k_rsem, True)
    send_part(2, v_buf.at[tok_rows(s), 0:HEAD], v_ssem, v_rsem.at[s], True)

    far_rows = group - tok

    def wait_part(ref, sem):
        pltpu.make_async_copy(ref, ref, sem).wait()

    wait_part(q_buf.at[0:far_rows], q_rsem)
    wait_part(c_buf.at[pl.ds(0, others)], c_rsem)

    @pl.loop(0, slots)
    def _(j):
        valid = j < used
        at = jnp.where(valid, list_ref[0, j], list_ref[0, 0]) // 2
        keep = jnp.where(valid, 1.0, 0.0).astype(jnp.float32)
        rows = pl.ds(pl.multiple_of(j * FTOK, FTOK), FTOK)
        k_all[rows, :] = c_buf[at, 0]
        v_all[rows, 0:HEAD] = (c_buf[at, 1].astype(jnp.float32) * keep).astype(jnp.bfloat16)
        v_all[rows, HEAD:2 * HEAD] = jnp.full((FTOK, HEAD), keep, jnp.float32).astype(jnp.bfloat16)

    top = jnp.full((group, 1), LOWEST, jnp.float32)
    acc[...] = jnp.zeros((group, 2 * HEAD), jnp.float32)
    scored[0] = rows_dot(q_buf[...], k_all[0:FTOK, :])
    for j in range(slots):
        keys = slice(j * FTOK, (j + 1) * FTOK)
        if j + 1 < slots:
            scored[(j + 1) % 2] = rows_dot(q_buf[...], k_all[(j + 1) * FTOK:(j + 2) * FTOK, :])
        scores = scored[j % 2]
        raised = jnp.maximum(top, jnp.max(scores, axis=1, keepdims=True))
        w = jnp.exp2((scores - raised) * RATE).astype(jnp.bfloat16)
        acc[...] = acc[...] * jnp.exp2((top - raised) * RATE) + jnp.dot(
            w, v_all[keys, :], preferred_element_type=jnp.float32)
        top = raised

    wait_part(k_buf.at[0:far_rows], k_rsem)

    def score_frame(f):
        own_scored[f % 2, :, 0:(f + 1) * FTOK] = rows_dot(
            q_buf[f * FTOK:(f + 1) * FTOK, :], k_buf[0:(f + 1) * FTOK, :])

    score_frame(0)
    for f in range(frames):
        if f + 1 < frames:
            score_frame(f + 1)
        rows, seen = slice(f * FTOK, (f + 1) * FTOK), (f + 1) * FTOK
        scores = own_scored[f % 2, :, 0:seen]
        raised = jnp.maximum(top[rows], jnp.max(scores, axis=1, keepdims=True))
        weights[rows, 0:seen] = jnp.exp2((scores - raised) * RATE).astype(jnp.bfloat16)
        acc[rows, :] = acc[rows, :] * jnp.exp2((top[rows] - raised) * RATE)

    waited = sent = 0
    for f in range(frames):
        rows, seen = slice(f * FTOK, (f + 1) * FTOK), (f + 1) * FTOK
        holders = -(-seen // tok)

        @pl.loop(waited, holders)
        def _(p):
            @pl.when(p != s)
            def _():
                wait_part(v_buf.at[tok_rows(p), 0:HEAD], v_rsem.at[p])

        total = acc[rows, :] + jnp.dot(weights[rows, 0:seen], v_buf[0:seen, :], preferred_element_type=jnp.float32)
        o_buf[rows, :] = (total[:, 0:HEAD] / total[:, HEAD:2 * HEAD]).astype(jnp.bfloat16)

        @pl.loop(0, seen // tok - sent)
        def _(i):
            p = sent + i

            @pl.when(p != s)
            def _():
                pltpu.make_async_remote_copy(o_buf.at[tok_rows(p), :], out_ref.at[:, head_cols(s)], o_ssem, o_rsem,
                                             device_id={"seq": p}, device_id_type=MESH).start()

        waited, sent = holders, seen // tok

    kept = pltpu.make_async_copy(o_buf.at[tok_rows(s), :], out_ref.at[:, head_cols(s)], own_sem.at[0])
    kept.start()
    kept.wait()
    wait_part(q_buf.at[0:far_rows], q_ssem)
    wait_part(k_buf.at[0:far_rows], k_ssem)
    wait_part(v_buf.at[0:far_rows, 0:HEAD], v_ssem)
    wait_part(c_buf.at[pl.ds(0, others)], c_ssem)
    wait_part(o_buf.at[0:far_rows], o_ssem)
    wait_part(o_buf.at[0:far_rows], o_rsem)


def solution(mesh):
    n_seq, n_cache = mesh.shape["seq"], mesh.shape["cache"]
    side = math.isqrt(n_cache)

    def shards(qkv, cache_kv, group_list, stream_counts):
        parts = jnp.transpose(qkv[0], (1, 0, 2))
        tok, width = parts.shape[1], parts.shape[2]
        slots = group_list.shape[1]
        group = tok * n_seq
        bf16, f32 = jnp.bfloat16, jnp.float32
        hbm = pl.BlockSpec(memory_space=pltpu.HBM)

        def body(*refs):
            kernel((n_seq, n_cache, tok, slots, side), *refs)

        out = pl.pallas_call(
            body,
            out_shape=pltpu.VMEM((tok, width), bf16),
            in_specs=[hbm, hbm, hbm, hbm],
            out_specs=pl.BlockSpec(memory_space=pltpu.VMEM),
            scratch_shapes=[
                pltpu.VMEM((group, HEAD), bf16),
                pltpu.VMEM((group, HEAD), bf16),
                pltpu.VMEM((group, 2 * HEAD), bf16),
                pltpu.VMEM((group, HEAD), bf16),
                pltpu.SMEM((1, slots), jnp.int32),
                pltpu.SMEM((1,), jnp.int32),
                pltpu.VMEM((8, 128), jnp.int32),
                pltpu.VMEM((n_cache, 8, 128), jnp.int32),
                pltpu.VMEM((2, 2, FTOK, HEAD), bf16),
                pltpu.VMEM((n_cache, 2, FTOK, HEAD), bf16),
                pltpu.VMEM((n_cache, 2, FTOK, HEAD), bf16),
                pltpu.VMEM((slots * FTOK, HEAD), bf16),
                pltpu.VMEM((slots * FTOK, 2 * HEAD), bf16),
                pltpu.VMEM((2, group, FTOK), f32),
                pltpu.VMEM((2, FTOK, group), f32),
                pltpu.VMEM((group, 2 * HEAD), f32),
                pltpu.VMEM((group, group), bf16),
            ] + [pltpu.SemaphoreType.DMA((6,))] + [pltpu.SemaphoreType.DMA] * 9 + [pltpu.SemaphoreType.DMA((n_seq,))]
            + [pltpu.SemaphoreType.DMA] * 2,
            compiler_params=pltpu.CompilerParams(
                collective_id=0, has_side_effects=True, vmem_limit_bytes=56 << 20),
            cost_estimate=pl.CostEstimate(
                flops=4 * group * (group + slots * FTOK) * HEAD,
                bytes_accessed=4 * tok * width * 2 + 4 * FTOK * HEAD * 2,
                transcendentals=group * (group + slots * FTOK)),
        )(group_list, stream_counts, parts, cache_kv)
        return out[None]

    placed = (
        P("cache", "seq", None, None),
        P("cache", None, None, "seq"),
        P("cache", None),
        P("cache"),
    )
    return jax.shard_map(
        shards, mesh=mesh, in_specs=placed, out_specs=P("cache", "seq", None), check_vma=False
    )
```

```python
import math

import jax
import jax.numpy as jnp
from jax import lax
from jax.experimental import pallas as pl
from jax.experimental.pallas import tpu as pltpu
from jax.sharding import PartitionSpec as P

HEAD = 128
FTOK = 256
MESH = pl.DeviceIdType.MESH
RATE = math.log2(math.e) / math.sqrt(HEAD)
LOWEST = -3.0e38


def rows_dot(a, b):
    return lax.dot_general(a, b, (((1,), (1,)), ((), ())), preferred_element_type=jnp.float32)


def kernel(sizes, list_hbm, count_hbm, x_ref, cache_ref, out_ref, q_buf, k_buf, v_buf, o_buf,
           list_ref, count_ref, note, notes, c_mine, c_send, c_buf, k_all, v_all, scored, own_scored, acc, weights,
           own_sem, note_ssem, note_rsem, c_ssem, c_rsem, q_ssem, q_rsem, k_ssem, k_rsem, v_ssem, v_rsem,
           o_ssem, o_rsem):
    n_seq, n_cache, tok, slots, side = sizes
    n_z = n_seq // 2
    s = lax.axis_index("seq")
    c = lax.axis_index("cache")
    z, core = s // 2, s % 2
    cy, cx = c // side, c % side
    group = n_seq * tok
    frames = group // FTOK

    half = n_z // 2

    def seq_peer(i):
        m = i // 2
        late = jnp.where(z >= half, 1, 0)
        j = m - late
        k, back = j // 2, j % 2
        wrapped = jnp.maximum(z - half, 0)
        ahead = jnp.where(k < wrapped, k, z + 1 + k - wrapped)
        behind = jnp.where(z >= half - 1, z - half + 1 + k, jnp.where(k < z, k, half + 1 + k))
        dest = jnp.where(back == 1, behind, ahead)
        dest = jnp.where(m == (1 - late) * (n_z - 2), lax.rem(z + half, n_z), dest)
        dest = jnp.where(m == n_z - 1, z, dest)
        return dest * 2 + lax.rem(core + i + 1, 2)

    def cache_peer(i):
        i = lax.rem(7 * i, n_cache)
        return lax.rem(cy + i // side, side) * side + lax.rem(cx + lax.rem(i, side), side)

    def head_cols(p):
        return pl.ds(pl.multiple_of(p * HEAD, HEAD), HEAD)

    def tok_rows(p):
        return pl.ds(pl.multiple_of(p * tok, 16), tok)

    barrier = pltpu.get_barrier_semaphore()

    @pl.loop(0, n_seq - 1)
    def _(i):
        pl.semaphore_signal(barrier, inc=1, device_id={"seq": seq_peer(i)}, device_id_type=MESH)

    @pl.loop(1, n_cache)
    def _(i):
        pl.semaphore_signal(barrier, inc=1, device_id={"cache": cache_peer(i)}, device_id_type=MESH)

    lists = [pltpu.make_async_copy(list_hbm, list_ref, own_sem.at[4]), pltpu.make_async_copy(count_hbm, count_ref, own_sem.at[5])]
    for copy in lists:
        copy.start()

    mine = [
        pltpu.make_async_copy(cache_ref, c_mine, own_sem.at[0]),
        pltpu.make_async_copy(x_ref.at[0, :, head_cols(s)], q_buf.at[tok_rows(s), :], own_sem.at[1]),
        pltpu.make_async_copy(x_ref.at[1, :, head_cols(s)], k_buf.at[tok_rows(s), :], own_sem.at[2]),
        pltpu.make_async_copy(x_ref.at[2, :, head_cols(s)], v_buf.at[tok_rows(s), 0:HEAD], own_sem.at[3]),
    ]
    for copy in mine:
        copy.start()

    for copy in lists:
        copy.wait()
    lanes = lax.broadcasted_iota(jnp.int32, (8, 128), 1)
    row = jnp.full((8, 128), -1, jnp.int32)
    used = count_ref[0]
    for j in range(slots):
        row = jnp.where(lanes == j, jnp.where(j < used, list_ref[0, j], -1), row)
    note[...] = row
    notes[c] = row
    v_buf[:, HEAD:2 * HEAD] = jnp.ones((group, HEAD), jnp.bfloat16)

    pl.semaphore_wait(barrier, n_seq - 1 + n_cache - 1)

    @pl.loop(1, n_cache)
    def _(i):
        pltpu.make_async_remote_copy(note, notes.at[c], note_ssem, note_rsem,
                                     device_id={"cache": cache_peer(i)}, device_id_type=MESH).start()

    def send_part(part, dst, ssem, rsem):
        @pl.loop(0, n_seq - 1)
        def _(i):
            p = seq_peer(i)
            pltpu.make_async_remote_copy(x_ref.at[part, :, head_cols(p)], dst, ssem, rsem,
                                         device_id={"seq": p}, device_id_type=MESH).start()

    send_part(0, q_buf.at[tok_rows(s), :], q_ssem, q_rsem)

    for copy in mine:
        copy.wait()
    others = n_cache - 1
    pltpu.make_async_copy(notes.at[pl.ds(0, others)], notes.at[pl.ds(0, others)], note_rsem).wait()
    pltpu.make_async_copy(notes.at[pl.ds(0, others)], notes.at[pl.ds(0, others)], note_ssem).wait()

    def listed(p):
        hit = jnp.where(notes[p] == 2 * c + 1, 1, 0)
        return jnp.max(hit)

    @pl.loop(1, n_cache)
    def _(i):
        p = cache_peer(i)
        c_send[p] = c_mine[listed(p)]
        pltpu.make_async_remote_copy(c_send.at[p], c_buf.at[c], c_ssem, c_rsem,
                                     device_id={"cache": p}, device_id_type=MESH).start()

    c_buf[c] = c_mine[listed(c)]
    send_part(1, k_buf.at[tok_rows(s), :], k_ssem, k_rsem)
    send_part(2, v_buf.at[tok_rows(s), 0:HEAD], v_ssem, v_rsem.at[s])

    far_rows = group - tok

    def wait_part(ref, sem):
        pltpu.make_async_copy(ref, ref, sem).wait()

    wait_part(q_buf.at[0:far_rows], q_rsem)
    wait_part(c_buf.at[pl.ds(0, others)], c_rsem)

    @pl.loop(0, slots)
    def _(j):
        valid = j < used
        at = jnp.where(valid, list_ref[0, j], list_ref[0, 0]) // 2
        keep = jnp.where(valid, 1.0, 0.0).astype(jnp.float32)
        rows = pl.ds(pl.multiple_of(j * FTOK, FTOK), FTOK)
        k_all[rows, :] = c_buf[at, 0]
        v_all[rows, 0:HEAD] = (c_buf[at, 1].astype(jnp.float32) * keep).astype(jnp.bfloat16)
        v_all[rows, HEAD:2 * HEAD] = jnp.full((FTOK, HEAD), keep, jnp.float32).astype(jnp.bfloat16)

    top = jnp.full((group, 1), LOWEST, jnp.float32)
    acc[...] = jnp.zeros((group, 2 * HEAD), jnp.float32)
    scored[0] = rows_dot(q_buf[...], k_all[0:FTOK, :])
    for j in range(slots):
        keys = slice(j * FTOK, (j + 1) * FTOK)
        if j + 1 < slots:
            scored[(j + 1) % 2] = rows_dot(q_buf[...], k_all[(j + 1) * FTOK:(j + 2) * FTOK, :])
        scores = scored[j % 2]
        raised = jnp.maximum(top, jnp.max(scores, axis=1, keepdims=True))
        w = jnp.exp2((scores - raised) * RATE).astype(jnp.bfloat16)
        acc[...] = acc[...] * jnp.exp2((top - raised) * RATE) + jnp.dot(
            w, v_all[keys, :], preferred_element_type=jnp.float32)
        top = raised

    wait_part(k_buf.at[0:far_rows], k_rsem)

    def score_frame(f):
        own_scored[f % 2, :, 0:(f + 1) * FTOK] = rows_dot(
            q_buf[f * FTOK:(f + 1) * FTOK, :], k_buf[0:(f + 1) * FTOK, :])

    score_frame(0)
    for f in range(frames):
        if f + 1 < frames:
            score_frame(f + 1)
        rows, seen = slice(f * FTOK, (f + 1) * FTOK), (f + 1) * FTOK
        scores = own_scored[f % 2, :, 0:seen]
        raised = jnp.maximum(top[rows], jnp.max(scores, axis=1, keepdims=True))
        weights[rows, 0:seen] = jnp.exp2((scores - raised) * RATE).astype(jnp.bfloat16)
        acc[rows, :] = acc[rows, :] * jnp.exp2((top[rows] - raised) * RATE)

    split = -(-(frames - 1) * FTOK // tok)
    plan = [(f, f * FTOK // tok, (f + 1) * FTOK // tok, False) for f in range(frames - 2)]
    plan += [(frames - 1, split, n_seq, True), (frames - 2, (frames - 2) * FTOK // tok, split, True)]
    waited = 0
    for f, low, high, descending in plan:
        rows, seen = slice(f * FTOK, (f + 1) * FTOK), (f + 1) * FTOK
        holders = max(waited, -(-seen // tok))

        @pl.loop(waited, holders)
        def _(p):
            @pl.when(p != s)
            def _():
                wait_part(v_buf.at[tok_rows(p), 0:HEAD], v_rsem.at[p])

        waited = holders
        total = acc[rows, :] + jnp.dot(weights[rows, 0:seen], v_buf[0:seen, :], preferred_element_type=jnp.float32)
        o_buf[rows, :] = (total[:, 0:HEAD] / total[:, HEAD:2 * HEAD]).astype(jnp.bfloat16)

        @pl.loop(low, high)
        def _(i):
            p = low + high - 1 - i if descending else i

            @pl.when(p != s)
            def _():
                pltpu.make_async_remote_copy(o_buf.at[tok_rows(p), :], out_ref.at[:, head_cols(s)], o_ssem, o_rsem,
                                             device_id={"seq": p}, device_id_type=MESH).start()

    kept = pltpu.make_async_copy(o_buf.at[tok_rows(s), :], out_ref.at[:, head_cols(s)], own_sem.at[0])
    kept.start()
    kept.wait()
    wait_part(q_buf.at[0:far_rows], q_ssem)
    wait_part(k_buf.at[0:far_rows], k_ssem)
    wait_part(v_buf.at[0:far_rows, 0:HEAD], v_ssem)
    wait_part(c_buf.at[pl.ds(0, others)], c_ssem)
    wait_part(o_buf.at[0:far_rows], o_ssem)
    wait_part(o_buf.at[0:far_rows], o_rsem)


def solution(mesh):
    n_seq, n_cache = mesh.shape["seq"], mesh.shape["cache"]
    side = math.isqrt(n_cache)

    def shards(qkv, cache_kv, group_list, stream_counts):
        parts = jnp.transpose(qkv[0], (1, 0, 2))
        tok, width = parts.shape[1], parts.shape[2]
        slots = group_list.shape[1]
        group = tok * n_seq
        bf16, f32 = jnp.bfloat16, jnp.float32
        hbm = pl.BlockSpec(memory_space=pltpu.HBM)

        def body(*refs):
            kernel((n_seq, n_cache, tok, slots, side), *refs)

        out = pl.pallas_call(
            body,
            out_shape=pltpu.VMEM((tok, width), bf16),
            in_specs=[hbm, hbm, hbm, hbm],
            out_specs=pl.BlockSpec(memory_space=pltpu.VMEM),
            scratch_shapes=[
                pltpu.VMEM((group, HEAD), bf16),
                pltpu.VMEM((group, HEAD), bf16),
                pltpu.VMEM((group, 2 * HEAD), bf16),
                pltpu.VMEM((group, HEAD), bf16),
                pltpu.SMEM((1, slots), jnp.int32),
                pltpu.SMEM((1,), jnp.int32),
                pltpu.VMEM((8, 128), jnp.int32),
                pltpu.VMEM((n_cache, 8, 128), jnp.int32),
                pltpu.VMEM((2, 2, FTOK, HEAD), bf16),
                pltpu.VMEM((n_cache, 2, FTOK, HEAD), bf16),
                pltpu.VMEM((n_cache, 2, FTOK, HEAD), bf16),
                pltpu.VMEM((slots * FTOK, HEAD), bf16),
                pltpu.VMEM((slots * FTOK, 2 * HEAD), bf16),
                pltpu.VMEM((2, group, FTOK), f32),
                pltpu.VMEM((2, FTOK, group), f32),
                pltpu.VMEM((group, 2 * HEAD), f32),
                pltpu.VMEM((group, group), bf16),
            ] + [pltpu.SemaphoreType.DMA((6,))] + [pltpu.SemaphoreType.DMA] * 9 + [pltpu.SemaphoreType.DMA((n_seq,))]
            + [pltpu.SemaphoreType.DMA] * 2,
            compiler_params=pltpu.CompilerParams(
                collective_id=0, has_side_effects=True, vmem_limit_bytes=56 << 20),
            cost_estimate=pl.CostEstimate(
                flops=4 * group * (group + slots * FTOK) * HEAD,
                bytes_accessed=4 * tok * width * 2 + 4 * FTOK * HEAD * 2,
                transcendentals=group * (group + slots * FTOK)),
        )(group_list, stream_counts, parts, cache_kv)
        return out[None]

    placed = (
        P("cache", "seq", None, None),
        P("cache", None, None, "seq"),
        P("cache", None),
        P("cache"),
    )
    return jax.shard_map(
        shards, mesh=mesh, in_specs=placed, out_specs=P("cache", "seq", None), check_vma=False
    )
```

```python
import math

import jax
import jax.numpy as jnp
from jax import lax
from jax.experimental import pallas as pl
from jax.experimental.pallas import tpu as pltpu
from jax.sharding import PartitionSpec as P

HEAD = 128
FTOK = 256
MESH = pl.DeviceIdType.MESH
RATE = math.log2(math.e) / math.sqrt(HEAD)
LOWEST = -3.0e38


def rows_dot(a, b):
    return lax.dot_general(a, b, (((1,), (1,)), ((), ())), preferred_element_type=jnp.float32)


def kernel(sizes, list_hbm, count_hbm, x_ref, cache_ref, out_ref, q_buf, k_buf, v_buf, o_buf,
           list_ref, count_ref, note, notes, c_mine, c_send, c_buf, k_all, v_all, scored, own_scored, acc, weights,
           own_sem, note_ssem, note_rsem, c_ssem, c_rsem, q_ssem, q_rsem, k_ssem, k_rsem, v_ssem, v_rsem,
           o_ssem, o_rsem):
    n_seq, n_cache, tok, slots, side = sizes
    n_z = n_seq // 2
    s = lax.axis_index("seq")
    c = lax.axis_index("cache")
    z, core = s // 2, s % 2
    cy, cx = c // side, c % side
    group = n_seq * tok
    frames = group // FTOK

    half = n_z // 2

    def seq_peer(i):
        m = i // 2
        late = jnp.where(z >= half, 1, 0)
        j = m - late
        k, back = j // 2, j % 2
        wrapped = jnp.maximum(z - half, 0)
        ahead = jnp.where(k < wrapped, k, z + 1 + k - wrapped)
        behind = jnp.where(z >= half - 1, z - half + 1 + k, jnp.where(k < z, k, half + 1 + k))
        dest = jnp.where(back == 1, behind, ahead)
        dest = jnp.where(m == (1 - late) * (n_z - 2), lax.rem(z + half, n_z), dest)
        dest = jnp.where(m == n_z - 1, z, dest)
        return dest * 2 + lax.rem(core + i + 1, 2)

    def cache_peer(i):
        i = lax.rem(7 * i, n_cache)
        return lax.rem(cy + i // side, side) * side + lax.rem(cx + lax.rem(i, side), side)

    def head_cols(p):
        return pl.ds(pl.multiple_of(p * HEAD, HEAD), HEAD)

    def tok_rows(p):
        return pl.ds(pl.multiple_of(p * tok, 16), tok)

    barrier = pltpu.get_barrier_semaphore()

    for i in range(n_seq - 1):
        p = jnp.where(i < s, i, i + 1)
        pl.semaphore_signal(barrier, inc=1, device_id={"seq": p}, device_id_type=MESH)

    @pl.loop(1, n_cache)
    def _(i):
        pl.semaphore_signal(barrier, inc=1, device_id={"cache": lax.rem(c + i, n_cache)}, device_id_type=MESH)

    pl.semaphore_wait(barrier, n_seq - 1 + n_cache - 1)

    def send_part(part, dst, ssem, rsem):
        @pl.loop(0, n_seq - 1)
        def _(i):
            p = seq_peer(i)
            pltpu.make_async_remote_copy(x_ref.at[part, :, head_cols(p)], dst, ssem, rsem,
                                         device_id={"seq": p}, device_id_type=MESH).start()

    send_part(0, q_buf.at[tok_rows(s), :], q_ssem, q_rsem)

    lists = [pltpu.make_async_copy(list_hbm, list_ref, own_sem.at[4]), pltpu.make_async_copy(count_hbm, count_ref, own_sem.at[5])]
    for copy in lists:
        copy.start()

    mine = [
        pltpu.make_async_copy(cache_ref, c_mine, own_sem.at[0]),
        pltpu.make_async_copy(x_ref.at[0, :, head_cols(s)], q_buf.at[tok_rows(s), :], own_sem.at[1]),
        pltpu.make_async_copy(x_ref.at[1, :, head_cols(s)], k_buf.at[tok_rows(s), :], own_sem.at[2]),
        pltpu.make_async_copy(x_ref.at[2, :, head_cols(s)], v_buf.at[tok_rows(s), 0:HEAD], own_sem.at[3]),
    ]
    for copy in mine:
        copy.start()

    for copy in lists:
        copy.wait()
    lanes = lax.broadcasted_iota(jnp.int32, (8, 128), 1)
    row = jnp.full((8, 128), -1, jnp.int32)
    used = count_ref[0]
    for j in range(slots):
        row = jnp.where(lanes == j, jnp.where(j < used, list_ref[0, j], -1), row)
    note[...] = row
    notes[c] = row

    @pl.loop(1, n_cache)
    def _(i):
        pltpu.make_async_remote_copy(note, notes.at[c], note_ssem, note_rsem,
                                     device_id={"cache": cache_peer(i)}, device_id_type=MESH).start()

    for copy in mine:
        copy.wait()
    others = n_cache - 1
    pltpu.make_async_copy(notes.at[pl.ds(0, others)], notes.at[pl.ds(0, others)], note_rsem).wait()
    pltpu.make_async_copy(notes.at[pl.ds(0, others)], notes.at[pl.ds(0, others)], note_ssem).wait()

    def listed(p):
        hit = jnp.where(notes[p] == 2 * c + 1, 1, 0)
        return jnp.max(hit)

    @pl.loop(1, n_cache)
    def _(i):
        p = cache_peer(i)
        c_send[p] = c_mine[listed(p)]
        pltpu.make_async_remote_copy(c_send.at[p], c_buf.at[c], c_ssem, c_rsem,
                                     device_id={"cache": p}, device_id_type=MESH).start()

    c_buf[c] = c_mine[listed(c)]
    send_part(1, k_buf.at[tok_rows(s), :], k_ssem, k_rsem)
    send_part(2, v_buf.at[tok_rows(s), 0:HEAD], v_ssem, v_rsem.at[s])

    v_buf[:, HEAD:2 * HEAD] = jnp.ones((group, HEAD), jnp.bfloat16)
    far_rows = group - tok

    def wait_part(ref, sem):
        pltpu.make_async_copy(ref, ref, sem).wait()

    wait_part(q_buf.at[0:far_rows], q_rsem)
    wait_part(c_buf.at[pl.ds(0, others)], c_rsem)

    @pl.loop(0, slots)
    def _(j):
        valid = j < used
        at = jnp.where(valid, list_ref[0, j], list_ref[0, 0]) // 2
        keep = jnp.where(valid, 1.0, 0.0).astype(jnp.float32)
        rows = pl.ds(pl.multiple_of(j * FTOK, FTOK), FTOK)
        k_all[rows, :] = c_buf[at, 0]
        v_all[rows, 0:HEAD] = (c_buf[at, 1].astype(jnp.float32) * keep).astype(jnp.bfloat16)
        v_all[rows, HEAD:2 * HEAD] = jnp.full((FTOK, HEAD), keep, jnp.float32).astype(jnp.bfloat16)

    top = jnp.full((group, 1), LOWEST, jnp.float32)
    acc[...] = jnp.zeros((group, 2 * HEAD), jnp.float32)
    scored[0] = rows_dot(q_buf[...], k_all[0:FTOK, :])
    for j in range(slots):
        keys = slice(j * FTOK, (j + 1) * FTOK)
        if j + 1 < slots:
            scored[(j + 1) % 2] = rows_dot(q_buf[...], k_all[(j + 1) * FTOK:(j + 2) * FTOK, :])
        scores = scored[j % 2]
        raised = jnp.maximum(top, jnp.max(scores, axis=1, keepdims=True))
        w = jnp.exp2((scores - raised) * RATE).astype(jnp.bfloat16)
        acc[...] = acc[...] * jnp.exp2((top - raised) * RATE) + jnp.dot(
            w, v_all[keys, :], preferred_element_type=jnp.float32)
        top = raised

    wait_part(k_buf.at[0:far_rows], k_rsem)

    def score_frame(f):
        own_scored[f % 2, :, 0:(f + 1) * FTOK] = rows_dot(
            q_buf[f * FTOK:(f + 1) * FTOK, :], k_buf[0:(f + 1) * FTOK, :])

    score_frame(0)
    for f in range(frames):
        if f + 1 < frames:
            score_frame(f + 1)
        rows, seen = slice(f * FTOK, (f + 1) * FTOK), (f + 1) * FTOK
        scores = own_scored[f % 2, :, 0:seen]
        raised = jnp.maximum(top[rows], jnp.max(scores, axis=1, keepdims=True))
        weights[rows, 0:seen] = jnp.exp2((scores - raised) * RATE).astype(jnp.bfloat16)
        acc[rows, :] = acc[rows, :] * jnp.exp2((top[rows] - raised) * RATE)

    split = -(-(frames - 1) * FTOK // tok)
    plan = [(f, f * FTOK // tok, (f + 1) * FTOK // tok, False) for f in range(frames - 2)]
    plan += [(frames - 1, split, n_seq, True), (frames - 2, (frames - 2) * FTOK // tok, split, True)]
    waited = 0
    for f, low, high, descending in plan:
        rows, seen = slice(f * FTOK, (f + 1) * FTOK), (f + 1) * FTOK
        holders = max(waited, -(-seen // tok))

        @pl.loop(waited, holders)
        def _(p):
            @pl.when(p != s)
            def _():
                wait_part(v_buf.at[tok_rows(p), 0:HEAD], v_rsem.at[p])

        waited = holders
        total = acc[rows, :] + jnp.dot(weights[rows, 0:seen], v_buf[0:seen, :], preferred_element_type=jnp.float32)
        o_buf[rows, :] = (total[:, 0:HEAD] / total[:, HEAD:2 * HEAD]).astype(jnp.bfloat16)

        @pl.loop(low, high)
        def _(i):
            p = low + high - 1 - i if descending else i

            @pl.when(p != s)
            def _():
                pltpu.make_async_remote_copy(o_buf.at[tok_rows(p), :], out_ref.at[:, head_cols(s)], o_ssem, o_rsem,
                                             device_id={"seq": p}, device_id_type=MESH).start()

    kept = pltpu.make_async_copy(o_buf.at[tok_rows(s), :], out_ref.at[:, head_cols(s)], own_sem.at[0])
    kept.start()
    kept.wait()
    wait_part(q_buf.at[0:far_rows], q_ssem)
    wait_part(k_buf.at[0:far_rows], k_ssem)
    wait_part(v_buf.at[0:far_rows, 0:HEAD], v_ssem)
    wait_part(c_buf.at[pl.ds(0, others)], c_ssem)
    wait_part(o_buf.at[0:far_rows], o_ssem)
    wait_part(o_buf.at[0:far_rows], o_rsem)


def solution(mesh):
    n_seq, n_cache = mesh.shape["seq"], mesh.shape["cache"]
    side = math.isqrt(n_cache)

    def shards(qkv, cache_kv, group_list, stream_counts):
        parts = jnp.transpose(qkv[0], (1, 0, 2))
        tok, width = parts.shape[1], parts.shape[2]
        slots = group_list.shape[1]
        group = tok * n_seq
        bf16, f32 = jnp.bfloat16, jnp.float32
        hbm = pl.BlockSpec(memory_space=pltpu.HBM)

        def body(*refs):
            kernel((n_seq, n_cache, tok, slots, side), *refs)

        out = pl.pallas_call(
            body,
            out_shape=pltpu.VMEM((tok, width), bf16),
            in_specs=[hbm, hbm, hbm, hbm],
            out_specs=pl.BlockSpec(memory_space=pltpu.VMEM),
            scratch_shapes=[
                pltpu.VMEM((group, HEAD), bf16),
                pltpu.VMEM((group, HEAD), bf16),
                pltpu.VMEM((group, 2 * HEAD), bf16),
                pltpu.VMEM((group, HEAD), bf16),
                pltpu.SMEM((1, slots), jnp.int32),
                pltpu.SMEM((1,), jnp.int32),
                pltpu.VMEM((8, 128), jnp.int32),
                pltpu.VMEM((n_cache, 8, 128), jnp.int32),
                pltpu.VMEM((2, 2, FTOK, HEAD), bf16),
                pltpu.VMEM((n_cache, 2, FTOK, HEAD), bf16),
                pltpu.VMEM((n_cache, 2, FTOK, HEAD), bf16),
                pltpu.VMEM((slots * FTOK, HEAD), bf16),
                pltpu.VMEM((slots * FTOK, 2 * HEAD), bf16),
                pltpu.VMEM((2, group, FTOK), f32),
                pltpu.VMEM((2, FTOK, group), f32),
                pltpu.VMEM((group, 2 * HEAD), f32),
                pltpu.VMEM((group, group), bf16),
            ] + [pltpu.SemaphoreType.DMA((6,))] + [pltpu.SemaphoreType.DMA] * 9 + [pltpu.SemaphoreType.DMA((n_seq,))]
            + [pltpu.SemaphoreType.DMA] * 2,
            compiler_params=pltpu.CompilerParams(
                collective_id=0, has_side_effects=True, vmem_limit_bytes=56 << 20),
            cost_estimate=pl.CostEstimate(
                flops=4 * group * (group + slots * FTOK) * HEAD,
                bytes_accessed=4 * tok * width * 2 + 4 * FTOK * HEAD * 2,
                transcendentals=group * (group + slots * FTOK)),
        )(group_list, stream_counts, parts, cache_kv)
        return out[None]

    placed = (
        P("cache", "seq", None, None),
        P("cache", None, None, "seq"),
        P("cache", None),
        P("cache"),
    )
    return jax.shard_map(
        shards, mesh=mesh, in_specs=placed, out_specs=P("cache", "seq", None), check_vma=False
    )
```

```python
import math

import jax
import jax.numpy as jnp
from jax import lax
from jax.experimental import pallas as pl
from jax.experimental.pallas import tpu as pltpu
from jax.sharding import PartitionSpec as P

HEAD = 128
FTOK = 256
MESH = pl.DeviceIdType.MESH
RATE = math.log2(math.e) / math.sqrt(HEAD)
LOWEST = -3.0e38


def rows_dot(a, b):
    return lax.dot_general(a, b, (((1,), (1,)), ((), ())), preferred_element_type=jnp.float32)


def kernel(sizes, list_hbm, count_hbm, x_ref, cache_ref, out_ref, q_buf, k_buf, v_buf, o_buf,
           list_ref, count_ref, note, notes, c_mine, c_send, c_buf, k_all, v_all, scored, own_scored, acc, weights,
           own_sem, note_ssem, note_rsem, c_ssem, c_rsem, q_ssem, q_rsem, k_ssem, k_rsem, v_ssem, v_rsem,
           o_ssem, o_rsem):
    n_seq, n_cache, tok, slots, side = sizes
    n_z = n_seq // 2
    s = lax.axis_index("seq")
    c = lax.axis_index("cache")
    z, core = s // 2, s % 2
    cy, cx = c // side, c % side
    group = n_seq * tok
    frames = group // FTOK

    half = n_z // 2

    def seq_peer(i):
        m = i // 2
        j = m - 1
        k, back = j // 2, j % 2
        wrapped = jnp.maximum(z - half, 0)
        ahead = jnp.where(k < wrapped, k, z + 1 + k - wrapped)
        behind = jnp.where(z >= half - 1, z - half + 1 + k, jnp.where(k < z, k, half + 1 + k))
        dest = jnp.where(back == 1, behind, ahead)
        dest = jnp.where(m == 0, lax.rem(z + half, n_z), dest)
        dest = jnp.where(m == n_z - 1, z, dest)
        return dest * 2 + lax.rem(core + i + 1, 2)

    def cache_peer(i):
        i = lax.rem(7 * i, n_cache)
        return lax.rem(cy + i // side, side) * side + lax.rem(cx + lax.rem(i, side), side)

    def head_cols(p):
        return pl.ds(pl.multiple_of(p * HEAD, HEAD), HEAD)

    def tok_rows(p):
        return pl.ds(pl.multiple_of(p * tok, 16), tok)

    barrier = pltpu.get_barrier_semaphore()

    for i in range(n_seq - 1):
        p = jnp.where(i < s, i, i + 1)
        pl.semaphore_signal(barrier, inc=1, device_id={"seq": p}, device_id_type=MESH)

    @pl.loop(1, n_cache)
    def _(i):
        pl.semaphore_signal(barrier, inc=1, device_id={"cache": lax.rem(c + i, n_cache)}, device_id_type=MESH)

    pl.semaphore_wait(barrier, n_seq - 1 + n_cache - 1)

    def send_part(part, dst, ssem, rsem):
        @pl.loop(0, n_seq - 1)
        def _(i):
            p = seq_peer(i)
            pltpu.make_async_remote_copy(x_ref.at[part, :, head_cols(p)], dst, ssem, rsem,
                                         device_id={"seq": p}, device_id_type=MESH).start()

    send_part(0, q_buf.at[tok_rows(s), :], q_ssem, q_rsem)

    lists = [pltpu.make_async_copy(list_hbm, list_ref, own_sem.at[4]), pltpu.make_async_copy(count_hbm, count_ref, own_sem.at[5])]
    for copy in lists:
        copy.start()

    mine = [
        pltpu.make_async_copy(cache_ref, c_mine, own_sem.at[0]),
        pltpu.make_async_copy(x_ref.at[0, :, head_cols(s)], q_buf.at[tok_rows(s), :], own_sem.at[1]),
        pltpu.make_async_copy(x_ref.at[1, :, head_cols(s)], k_buf.at[tok_rows(s), :], own_sem.at[2]),
        pltpu.make_async_copy(x_ref.at[2, :, head_cols(s)], v_buf.at[tok_rows(s), 0:HEAD], own_sem.at[3]),
    ]
    for copy in mine:
        copy.start()

    for copy in lists:
        copy.wait()
    lanes = lax.broadcasted_iota(jnp.int32, (8, 128), 1)
    row = jnp.full((8, 128), -1, jnp.int32)
    used = count_ref[0]
    for j in range(slots):
        row = jnp.where(lanes == j, jnp.where(j < used, list_ref[0, j], -1), row)
    note[...] = row
    notes[c] = row

    @pl.loop(1, n_cache)
    def _(i):
        pltpu.make_async_remote_copy(note, notes.at[c], note_ssem, note_rsem,
                                     device_id={"cache": cache_peer(i)}, device_id_type=MESH).start()

    for copy in mine:
        copy.wait()
    others = n_cache - 1
    pltpu.make_async_copy(notes.at[pl.ds(0, others)], notes.at[pl.ds(0, others)], note_rsem).wait()
    pltpu.make_async_copy(notes.at[pl.ds(0, others)], notes.at[pl.ds(0, others)], note_ssem).wait()

    def listed(p):
        hit = jnp.where(notes[p] == 2 * c + 1, 1, 0)
        return jnp.max(hit)

    @pl.loop(1, n_cache)
    def _(i):
        p = cache_peer(i)
        c_send[p] = c_mine[listed(p)]
        pltpu.make_async_remote_copy(c_send.at[p], c_buf.at[c], c_ssem, c_rsem,
                                     device_id={"cache": p}, device_id_type=MESH).start()

    c_buf[c] = c_mine[listed(c)]
    send_part(1, k_buf.at[tok_rows(s), :], k_ssem, k_rsem)
    send_part(2, v_buf.at[tok_rows(s), 0:HEAD], v_ssem, v_rsem.at[s])

    v_buf[:, HEAD:2 * HEAD] = jnp.ones((group, HEAD), jnp.bfloat16)
    far_rows = group - tok

    def wait_part(ref, sem):
        pltpu.make_async_copy(ref, ref, sem).wait()

    wait_part(q_buf.at[0:far_rows], q_rsem)
    wait_part(c_buf.at[pl.ds(0, others)], c_rsem)

    @pl.loop(0, slots)
    def _(j):
        valid = j < used
        at = jnp.where(valid, list_ref[0, j], list_ref[0, 0]) // 2
        keep = jnp.where(valid, 1.0, 0.0).astype(jnp.float32)
        rows = pl.ds(pl.multiple_of(j * FTOK, FTOK), FTOK)
        k_all[rows, :] = c_buf[at, 0]
        v_all[rows, 0:HEAD] = (c_buf[at, 1].astype(jnp.float32) * keep).astype(jnp.bfloat16)
        v_all[rows, HEAD:2 * HEAD] = jnp.full((FTOK, HEAD), keep, jnp.float32).astype(jnp.bfloat16)

    top = jnp.full((group, 1), LOWEST, jnp.float32)
    acc[...] = jnp.zeros((group, 2 * HEAD), jnp.float32)
    scored[0] = rows_dot(q_buf[...], k_all[0:FTOK, :])
    for j in range(slots):
        keys = slice(j * FTOK, (j + 1) * FTOK)
        if j + 1 < slots:
            scored[(j + 1) % 2] = rows_dot(q_buf[...], k_all[(j + 1) * FTOK:(j + 2) * FTOK, :])
        scores = scored[j % 2]
        raised = jnp.maximum(top, jnp.max(scores, axis=1, keepdims=True))
        w = jnp.exp2((scores - raised) * RATE).astype(jnp.bfloat16)
        acc[...] = acc[...] * jnp.exp2((top - raised) * RATE) + jnp.dot(
            w, v_all[keys, :], preferred_element_type=jnp.float32)
        top = raised

    wait_part(k_buf.at[0:far_rows], k_rsem)

    def score_frame(f):
        own_scored[f % 2, :, 0:(f + 1) * FTOK] = rows_dot(
            q_buf[f * FTOK:(f + 1) * FTOK, :], k_buf[0:(f + 1) * FTOK, :])

    score_frame(0)
    for f in range(frames):
        if f + 1 < frames:
            score_frame(f + 1)
        rows, seen = slice(f * FTOK, (f + 1) * FTOK), (f + 1) * FTOK
        scores = own_scored[f % 2, :, 0:seen]
        raised = jnp.maximum(top[rows], jnp.max(scores, axis=1, keepdims=True))
        weights[rows, 0:seen] = jnp.exp2((scores - raised) * RATE).astype(jnp.bfloat16)
        acc[rows, :] = acc[rows, :] * jnp.exp2((top[rows] - raised) * RATE)

    split = -(-(frames - 1) * FTOK // tok)
    plan = [(f, f * FTOK // tok, (f + 1) * FTOK // tok, False) for f in range(frames - 2)]
    plan += [(frames - 1, split, n_seq, True), (frames - 2, (frames - 2) * FTOK // tok, split, True)]
    waited = 0
    for f, low, high, descending in plan:
        rows, seen = slice(f * FTOK, (f + 1) * FTOK), (f + 1) * FTOK
        holders = max(waited, -(-seen // tok))

        @pl.loop(waited, holders)
        def _(p):
            @pl.when(p != s)
            def _():
                wait_part(v_buf.at[tok_rows(p), 0:HEAD], v_rsem.at[p])

        waited = holders
        total = acc[rows, :] + jnp.dot(weights[rows, 0:seen], v_buf[0:seen, :], preferred_element_type=jnp.float32)
        o_buf[rows, :] = (total[:, 0:HEAD] / total[:, HEAD:2 * HEAD]).astype(jnp.bfloat16)

        @pl.loop(low, high)
        def _(i):
            p = low + high - 1 - i if descending else i

            @pl.when(p != s)
            def _():
                pltpu.make_async_remote_copy(o_buf.at[tok_rows(p), :], out_ref.at[:, head_cols(s)], o_ssem, o_rsem,
                                             device_id={"seq": p}, device_id_type=MESH).start()

    kept = pltpu.make_async_copy(o_buf.at[tok_rows(s), :], out_ref.at[:, head_cols(s)], own_sem.at[0])
    kept.start()
    kept.wait()
    wait_part(q_buf.at[0:far_rows], q_ssem)
    wait_part(k_buf.at[0:far_rows], k_ssem)
    wait_part(v_buf.at[0:far_rows, 0:HEAD], v_ssem)
    wait_part(c_buf.at[pl.ds(0, others)], c_ssem)
    wait_part(o_buf.at[0:far_rows], o_ssem)
    wait_part(o_buf.at[0:far_rows], o_rsem)


def solution(mesh):
    n_seq, n_cache = mesh.shape["seq"], mesh.shape["cache"]
    side = math.isqrt(n_cache)

    def shards(qkv, cache_kv, group_list, stream_counts):
        parts = jnp.transpose(qkv[0], (1, 0, 2))
        tok, width = parts.shape[1], parts.shape[2]
        slots = group_list.shape[1]
        group = tok * n_seq
        bf16, f32 = jnp.bfloat16, jnp.float32
        hbm = pl.BlockSpec(memory_space=pltpu.HBM)

        def body(*refs):
            kernel((n_seq, n_cache, tok, slots, side), *refs)

        out = pl.pallas_call(
            body,
            out_shape=pltpu.VMEM((tok, width), bf16),
            in_specs=[hbm, hbm, hbm, hbm],
            out_specs=pl.BlockSpec(memory_space=pltpu.VMEM),
            scratch_shapes=[
                pltpu.VMEM((group, HEAD), bf16),
                pltpu.VMEM((group, HEAD), bf16),
                pltpu.VMEM((group, 2 * HEAD), bf16),
                pltpu.VMEM((group, HEAD), bf16),
                pltpu.SMEM((1, slots), jnp.int32),
                pltpu.SMEM((1,), jnp.int32),
                pltpu.VMEM((8, 128), jnp.int32),
                pltpu.VMEM((n_cache, 8, 128), jnp.int32),
                pltpu.VMEM((2, 2, FTOK, HEAD), bf16),
                pltpu.VMEM((n_cache, 2, FTOK, HEAD), bf16),
                pltpu.VMEM((n_cache, 2, FTOK, HEAD), bf16),
                pltpu.VMEM((slots * FTOK, HEAD), bf16),
                pltpu.VMEM((slots * FTOK, 2 * HEAD), bf16),
                pltpu.VMEM((2, group, FTOK), f32),
                pltpu.VMEM((2, FTOK, group), f32),
                pltpu.VMEM((group, 2 * HEAD), f32),
                pltpu.VMEM((group, group), bf16),
            ] + [pltpu.SemaphoreType.DMA((6,))] + [pltpu.SemaphoreType.DMA] * 9 + [pltpu.SemaphoreType.DMA((n_seq,))]
            + [pltpu.SemaphoreType.DMA] * 2,
            compiler_params=pltpu.CompilerParams(
                collective_id=0, has_side_effects=True, vmem_limit_bytes=56 << 20),
            cost_estimate=pl.CostEstimate(
                flops=4 * group * (group + slots * FTOK) * HEAD,
                bytes_accessed=4 * tok * width * 2 + 4 * FTOK * HEAD * 2,
                transcendentals=group * (group + slots * FTOK)),
        )(group_list, stream_counts, parts, cache_kv)
        return out[None]

    placed = (
        P("cache", "seq", None, None),
        P("cache", None, None, "seq"),
        P("cache", None),
        P("cache"),
    )
    return jax.shard_map(
        shards, mesh=mesh, in_specs=placed, out_specs=P("cache", "seq", None), check_vma=False
    )
```
